512 devices in a mesh: dp: 16 (over x, y_hi, core), mp: 32 (over y_lo, z).
Axes of the slice: x: 4, y: 8 (y_hi: 2, y_lo: 4; y = y_hi * 4 + y_lo), z: 8, core: 2. Of those that a mesh axis runs over, the one named last changes fastest.
Arguments:
- tokens: bfloat16 [5120, 3072], P(('dp', 'mp')), parts along dimension 0, may hold values from -6 to 6
- w_input: bfloat16 [3072, 12288], P(None, 'mp'), may hold values from -0.109375 to 0.109375
- b_input: float32 [12288], P('mp'), may hold values from -3 to 3
- w_output: bfloat16 [12288, 3072], P('mp'), may hold values from -0.0546875 to 0.0546875
- b_output: float32 [3072], replicated, may hold values from -3 to 3
Outputs:
- mlp_out: float32 [5120, 3072], P(('dp', 'mp')), parts along dimension 0
The draws below stay inside these ranges and needn't reach their ends.
There are 16 independent parts, one for each index of `dp`. The reference program is written for one: setup_inputs(seed, part) draws one part's arguments, and reference() takes and returns one part's arrays. A program takes and returns all parts, laid end to end along the dimension named above; an argument that names none is the same for every part. Nothing has to cross between parts.
All inputs are finite; a program needn't handle non-finite values.
Results may differ from the reference program's by a relative error of at most 0.0024.
Values may be sent and summed in bfloat16 or wider, within the bound.
No kernel may reach another device: no remote copies, remote signals or barrier semaphores. Data moves between devices by JAX's collectives and lax.ppermute only.
A program may use at most 64 MiB of HBM per device.

```python
import jax
import jax.numpy as jnp

D = 3072
FF = 12288
TOKENS = 320


def shard_levels(own_key, shape, split, low, high):
    def one(axis_at, shards_of):
        draws = jax.random.uniform(jax.random.fold_in(jax.random.fold_in(own_key, 6), axis_at), (shards_of,), jnp.float32, low / len(split), high / len(split))
        return jnp.repeat(jnp.exp(draws), shape[axis_at] // shards_of).reshape((-1,) + (1,) * (len(shape) - axis_at - 1))

    loudness = one(*split[0])
    for cut in split[1:]:
        loudness = loudness * one(*cut)
    return loudness


def scatter_about(rng, shape, deviation, most, split=(), kind=jnp.bfloat16):
    result = deviation * jax.random.normal(rng, shape, jnp.float32)
    if split:
        result = result * shard_levels(rng, shape, split, -0.22, 0.18)
    return jnp.clip(result, -most, most).astype(kind)


def setup_inputs(seed: int = 0, part: int = 0) -> dict:
    key_of = jax.random.split(jax.random.key(seed), 6)
    part_splits = jax.random.split(jax.random.fold_in(key_of[5], part), 6)
    return {
        "tokens": scatter_about(part_splits[0], (TOKENS, D), 1.0, 6.0, ((0, 32),)),
        "w_input": scatter_about(key_of[1], (D, FF), D ** -0.5, 0.109375, ((1, 32),)),
        "b_input": scatter_about(key_of[2], (FF,), 0.5, 3.0, ((0, 32),), jnp.float32),
        "w_output": scatter_about(key_of[3], (FF, D), FF ** -0.5, 0.0546875, ((0, 32),)),
        "b_output": scatter_about(key_of[4], (D,), 0.5, 3.0, (), jnp.float32),
    }


def reference(tokens, w_input, b_input, w_output, b_output):
    pre = jnp.dot(tokens, w_input, preferred_element_type=jnp.float32) + b_input
    hidden = jax.nn.gelu(pre, approximate=False).astype(jnp.bfloat16)
    total = jnp.dot(hidden, w_output, preferred_element_type=jnp.float32)
    return total + b_output
```

```python
import jax
import jax.numpy as jnp
from jax import lax
from jax.sharding import Mesh, PartitionSpec as P

X, YH, CORES, YL, Z = 4, 2, 2, 4, 8
Y = YH * YL
NAMES = ("x", "y_hi", "core", "y_lo", "z")


def pairs(step):
    out = []
    for i in range(X * Y * CORES * Z):
        rest, z = divmod(i, Z)
        rest, yl = divmod(rest, YL)
        rest, core = divmod(rest, CORES)
        x, yh = divmod(rest, YH)
        x2, y2, c2, z2 = step(x, yh * YL + yl, core, z)
        yh2, yl2 = divmod(y2 % Y, YL)
        out.append((i, (((x2 * YH + yh2) * CORES + c2) * YL + yl2) * Z + z2 % Z))
    return out


def along_y(k):
    return pairs(lambda x, y, c, z: (x, y + k * (1 - 2 * c), c, z))


def body(tokens, w_input, b_input, w_output, b_output):
    rows = tokens.shape[0]
    mine = lax.all_gather(tokens, "z", axis=0, tiled=True)

    def mlp(block):
        pre = jnp.dot(block, w_input, preferred_element_type=jnp.float32) + b_input
        hidden = jax.nn.gelu(pre, approximate=False).astype(jnp.bfloat16)
        return jnp.dot(hidden, w_output, preferred_element_type=jnp.float32)

    hops = (2, 1, -1)
    away = [lax.ppermute(mine, NAMES, along_y(k)) for k in hops]
    total = mlp(mine)
    back = [
        lax.ppermute(mlp(block).astype(jnp.bfloat16), NAMES, along_y(-k))
        for block, k in zip(away, hops)
    ]
    for part in back:
        total = total + part.astype(jnp.float32)
    total = total.reshape(Z, rows, -1)
    me = lax.axis_index("z")
    own = lax.dynamic_index_in_dim(total, me, 0, keepdims=True)
    got = lax.all_to_all(total.astype(jnp.bfloat16), "z", 0, 0, tiled=True)
    at = lax.broadcasted_iota(jnp.int32, (Z, 1, 1), 0)
    summed = jnp.where(at == me, own, got.astype(jnp.float32)).sum(0)
    return summed + b_output


def solution(mesh):
    fine = Mesh(mesh.devices.reshape(X, YH, CORES, YL, Z), NAMES)
    mp = ("y_lo", "z")
    return jax.shard_map(
        body,
        mesh=fine,
        in_specs=(P(NAMES, None), P(None, mp), P(mp), P(mp, None), P()),
        out_specs=P(NAMES, None),
        check_vma=False,
    )
```

```python
import jax
import jax.numpy as jnp
from jax import lax
from jax.experimental import pallas as pl
from jax.experimental.pallas import tpu as pltpu
from jax.sharding import Mesh, PartitionSpec as P

X, YH, CORES, YL, Z = 4, 2, 2, 4, 8
Y = YH * YL
NAMES = ("x", "y_hi", "core", "y_lo", "z")

EIGHT, REST, QUARTERS = 8, 2, 4
MAIN, LEFT = EIGHT * Z, REST * Z


def pairs(step):
    out = []
    for i in range(X * Y * CORES * Z):
        rest, z = divmod(i, Z)
        rest, yl = divmod(rest, YL)
        rest, core = divmod(rest, CORES)
        x, yh = divmod(rest, YH)
        x2, y2, c2, z2 = step(x, yh * YL + yl, core, z)
        yh2, yl2 = divmod(y2 % Y, YL)
        out.append((i, (((x2 * YH + yh2) * CORES + c2) * YL + yl2) * Z + z2 % Z))
    return out


def along_y(block, k):
    return lax.ppermute(block, NAMES, pairs(lambda x, y, c, z: (x, y + k * (1 - 2 * c), c, z)))


def exchange_z(blocks):
    return lax.all_to_all(blocks.reshape(Z, EIGHT, -1), "z", 0, 0, tiled=True).reshape(MAIN, -1)


def picks(q):
    row = lax.broadcasted_iota(jnp.int32, (LEFT, MAIN), 0)
    col = lax.broadcasted_iota(jnp.int32, (LEFT, MAIN), 1)
    return (col == QUARTERS * row + q).astype(jnp.bfloat16)


def puts(q):
    row = lax.broadcasted_iota(jnp.int32, (MAIN, LEFT), 0)
    col = lax.broadcasted_iota(jnp.int32, (MAIN, LEFT), 1)
    return (row == QUARTERS * col + q).astype(jnp.bfloat16)


def dot(a, b):
    return jnp.dot(a, b, preferred_element_type=jnp.float32)


def copies_kernel(tokens, out):
    features = tokens.shape[1]
    part = features // QUARTERS
    rows = tokens[...].astype(jnp.float32)
    rest = [
        rows[EIGHT + r : EIGHT + r + 1, q * part : (q + 1) * part] for r in range(REST) for q in range(QUARTERS)
    ]
    out[:, :features] = jnp.concatenate([rows[:EIGHT]] * Z, 0).astype(jnp.bfloat16)
    out[:, features:] = jnp.concatenate(rest * Z, 0).astype(jnp.bfloat16)


def hidden_of(packed, w_input, b_input, block):
    features = w_input.shape[0]
    part = features // QUARTERS
    block[:MAIN] = packed[:, :features]
    left = packed[:, features:]
    for q in range(QUARTERS):
        block[MAIN:, q * part : (q + 1) * part] = dot(picks(q), left).astype(jnp.bfloat16)
    pre = dot(block[...], w_input[...]) + b_input[...]
    return (0.5 * pre * (1.0 + lax.erf(pre * (0.5**0.5)))).astype(jnp.bfloat16)


def away_kernel(packed, w_input, b_input, w_output, out, block):
    hidden = hidden_of(packed, w_input, b_input, block)
    features = w_output.shape[1]
    part = features // QUARTERS
    left = jnp.zeros((MAIN, part), jnp.float32)
    for q in range(QUARTERS):
        at = slice(q * part, (q + 1) * part)
        sums = dot(hidden, w_output[:, at])
        out[:, at] = sums[:MAIN].astype(jnp.bfloat16)
        left = left + dot(puts(q), sums[MAIN:].astype(jnp.bfloat16))
    out[:, features:] = left.astype(jnp.bfloat16)


def own_kernel(packed, w_input, b_input, w_output, out, block):
    hidden = hidden_of(packed, w_input, b_input, block)
    part = w_output.shape[1] // QUARTERS
    for q in range(QUARTERS):
        at = slice(q * part, (q + 1) * part)
        out[:, at] = dot(hidden, w_output[:, at])


def add_kernel(own, one, two, three, total, packed):
    features = own.shape[1]
    part = features // QUARTERS
    terms = (one, two, three)
    main = own[:MAIN]
    for term in terms:
        main = main + term[:, :features].astype(jnp.float32)
    total[:MAIN] = main
    packed[:, :features] = main.astype(jnp.bfloat16)
    left = jnp.zeros((MAIN, part), jnp.float32)
    for q in range(QUARTERS):
        at = slice(q * part, (q + 1) * part)
        sums = own[MAIN:, at]
        for term in terms:
            sums = sums + dot(picks(q), term[:, features:])
        total[MAIN:, at] = sums
        left = left + dot(puts(q), sums.astype(jnp.bfloat16))
    packed[:, features:] = left.astype(jnp.bfloat16)


def last_kernel(total, got, b_output, out):
    features = total.shape[1]
    part = features // QUARTERS
    me = lax.axis_index("z")
    bias = b_output[...]
    summed = jnp.zeros((EIGHT, got.shape[1]), jnp.float32)
    others = got[...].astype(jnp.float32)
    for z in range(Z):
        summed = summed + jnp.where(me == z, 0.0, others[z * EIGHT : (z + 1) * EIGHT])
    at = pl.multiple_of(me * EIGHT, EIGHT)
    out[:EIGHT] = summed[:, :features] + total[pl.ds(at, EIGHT)] + bias
    rows = lax.broadcasted_iota(jnp.int32, (LEFT, 1), 0)
    for r in range(REST):
        mine = jnp.where(rows == me * REST + r, total[MAIN:], 0.0).sum(0, keepdims=True) + bias
        for q in range(QUARTERS):
            cols = slice(q * part, (q + 1) * part)
            row = QUARTERS * r + q
            out[EIGHT + r : EIGHT + r + 1, cols] = mine[:, cols] + summed[row : row + 1, features:]


def call(kernel, outs, args, scratch=(), flops=0):
    moved = sum(a.size * a.dtype.itemsize for a in args) + sum(o.size * o.dtype.itemsize for o in outs)
    return pl.pallas_call(
        kernel,
        out_shape=outs,
        in_specs=[pl.BlockSpec(memory_space=pltpu.VMEM)] * len(args),
        out_specs=tuple(pl.BlockSpec(memory_space=pltpu.VMEM) for _ in outs),
        scratch_shapes=scratch,
        compiler_params=pltpu.CompilerParams(vmem_limit_bytes=32 << 20),
        cost_estimate=pl.CostEstimate(flops=flops, bytes_accessed=moved, transcendentals=0),
    )(*args)


def body(tokens, w_input, b_input, w_output, b_output):
    features, units = w_input.shape
    wide = features + features // QUARTERS
    rows = MAIN + LEFT
    weights = (w_input, b_input.reshape(1, -1), w_output)
    packed = jax.ShapeDtypeStruct((MAIN, wide), jnp.bfloat16)
    sums = jax.ShapeDtypeStruct((rows, features), jnp.float32)
    block = (pltpu.VMEM((rows, features), jnp.bfloat16),)
    flops = 4 * rows * features * units

    (copies,) = call(copies_kernel, (packed,), (tokens,))
    mine = exchange_z(copies)
    up1 = along_y(mine, 1)
    (own,) = call(own_kernel, (sums,), (mine,) + weights, block, flops)
    up2 = along_y(up1, 1)
    down1 = along_y(mine, -1)
    back = []
    for away, k in ((up1, -1), (down1, 1), (up2, -2)):
        (part,) = call(away_kernel, (packed,), (away,) + weights, block, flops)
        back.append(along_y(part, k))
    total, outgoing = call(add_kernel, (sums, packed), (own, *back))
    got = exchange_z(outgoing)
    (out,) = call(
        last_kernel,
        (jax.ShapeDtypeStruct((EIGHT + REST, features), jnp.float32),),
        (total, got, b_output.reshape(1, -1)),
    )
    return out


def solution(mesh):
    fine = Mesh(mesh.devices.reshape(X, YH, CORES, YL, Z), NAMES)
    mp = ("y_lo", "z")
    return jax.shard_map(
        body,
        mesh=fine,
        in_specs=(P(NAMES, None), P(None, mp), P(mp), P(mp, None), P()),
        out_specs=P(NAMES, None),
        check_vma=False,
    )
```

```python
import jax
import jax.numpy as jnp
from jax import lax
from jax.experimental import pallas as pl
from jax.experimental.pallas import tpu as pltpu
from jax.sharding import Mesh, PartitionSpec as P

X, YH, CORES, YL, Z = 4, 2, 2, 4, 8
Y = YH * YL
NAMES = ("x", "y_hi", "core", "y_lo", "z")

EIGHT, REST, QUARTERS = 8, 2, 4
MAIN, LEFT = EIGHT * Z, REST * Z


def pairs(step):
    out = []
    for i in range(X * Y * CORES * Z):
        rest, z = divmod(i, Z)
        rest, yl = divmod(rest, YL)
        rest, core = divmod(rest, CORES)
        x, yh = divmod(rest, YH)
        x2, y2, c2, z2 = step(x, yh * YL + yl, core, z)
        yh2, yl2 = divmod(y2 % Y, YL)
        out.append((i, (((x2 * YH + yh2) * CORES + c2) * YL + yl2) * Z + z2 % Z))
    return out


def along_y(block, k):
    return lax.ppermute(block, NAMES, pairs(lambda x, y, c, z: (x, y + k * (1 - 2 * c), c, z)))


def exchange_z(blocks):
    return lax.all_to_all(blocks.reshape(Z, EIGHT, -1), "z", 0, 0, tiled=True).reshape(MAIN, -1)


def picks(q):
    row = lax.broadcasted_iota(jnp.int32, (LEFT, MAIN), 0)
    col = lax.broadcasted_iota(jnp.int32, (LEFT, MAIN), 1)
    return (col == QUARTERS * row + q).astype(jnp.bfloat16)


def puts(q):
    row = lax.broadcasted_iota(jnp.int32, (MAIN, LEFT), 0)
    col = lax.broadcasted_iota(jnp.int32, (MAIN, LEFT), 1)
    return (row == QUARTERS * col + q).astype(jnp.bfloat16)


def dot(a, b):
    return jnp.dot(a, b, preferred_element_type=jnp.float32)


def copies_kernel(tokens, out):
    features = tokens.shape[1]
    part = features // QUARTERS
    rows = tokens[...].astype(jnp.float32)
    rest = [
        rows[EIGHT + r : EIGHT + r + 1, q * part : (q + 1) * part] for r in range(REST) for q in range(QUARTERS)
    ]
    out[:, :features] = jnp.concatenate([rows[:EIGHT]] * Z, 0).astype(jnp.bfloat16)
    out[:, features:] = jnp.concatenate(rest * Z, 0).astype(jnp.bfloat16)


def hidden_of(packed, w_input, b_input, block):
    features = w_input.shape[0]
    part = features // QUARTERS
    block[:MAIN] = packed[:, :features]
    left = packed[:, features:]
    for q in range(QUARTERS):
        block[MAIN:, q * part : (q + 1) * part] = dot(picks(q), left).astype(jnp.bfloat16)
    pre = dot(block[...], w_input[...]) + b_input[...].reshape(1, -1)
    return (0.5 * pre * (1.0 + lax.erf(pre * (0.5**0.5)))).astype(jnp.bfloat16)


def away_kernel(packed, w_input, b_input, w_output, earlier, out, block):
    hidden = hidden_of(packed, w_input, b_input, block)
    features = w_output.shape[1]
    part = features // QUARTERS
    left = jnp.zeros((MAIN, part), jnp.float32)
    for q in range(QUARTERS):
        at = slice(q * part, (q + 1) * part)
        sums = dot(hidden, w_output[:, at])
        out[:, at] = sums[:MAIN].astype(jnp.bfloat16)
        left = left + dot(puts(q), sums[MAIN:].astype(jnp.bfloat16))
    out[:, features:] = left.astype(jnp.bfloat16)


def own_kernel(packed, w_input, b_input, w_output, out, block):
    hidden = hidden_of(packed, w_input, b_input, block)
    part = w_output.shape[1] // QUARTERS
    for q in range(QUARTERS):
        at = slice(q * part, (q + 1) * part)
        out[:, at] = dot(hidden, w_output[:, at])


def add_kernel(own, one, two, three, total, packed):
    features = own.shape[1]
    part = features // QUARTERS
    terms = (one, two, three)
    main = own[:MAIN]
    for term in terms:
        main = main + term[:, :features].astype(jnp.float32)
    total[:MAIN] = main
    packed[:, :features] = main.astype(jnp.bfloat16)
    left = jnp.zeros((MAIN, part), jnp.float32)
    for q in range(QUARTERS):
        at = slice(q * part, (q + 1) * part)
        sums = own[MAIN:, at]
        for term in terms:
            sums = sums + dot(picks(q), term[:, features:])
        total[MAIN:, at] = sums
        left = left + dot(puts(q), sums.astype(jnp.bfloat16))
    packed[:, features:] = left.astype(jnp.bfloat16)


def last_kernel(total, got, b_output, out):
    features = total.shape[1]
    part = features // QUARTERS
    me = lax.axis_index("z")
    bias = b_output[...].reshape(1, -1)
    summed = jnp.zeros((EIGHT, got.shape[1]), jnp.float32)
    others = got[...].astype(jnp.float32)
    for z in range(Z):
        summed = summed + jnp.where(me == z, 0.0, others[z * EIGHT : (z + 1) * EIGHT])
    at = pl.multiple_of(me * EIGHT, EIGHT)
    out[:EIGHT] = summed[:, :features] + total[pl.ds(at, EIGHT)] + bias
    rows = lax.broadcasted_iota(jnp.int32, (LEFT, 1), 0)
    for r in range(REST):
        mine = jnp.where(rows == me * REST + r, total[MAIN:], 0.0).sum(0, keepdims=True) + bias
        for q in range(QUARTERS):
            cols = slice(q * part, (q + 1) * part)
            row = QUARTERS * r + q
            out[EIGHT + r : EIGHT + r + 1, cols] = mine[:, cols] + summed[row : row + 1, features:]


def call(kernel, outs, args, scratch=(), flops=0, after=()):
    moved = sum(a.size * a.dtype.itemsize for a in args) + sum(o.size * o.dtype.itemsize for o in outs)
    return pl.pallas_call(
        kernel,
        out_shape=outs,
        in_specs=[pl.BlockSpec(memory_space=pltpu.VMEM)] * len(args) + [pl.BlockSpec(memory_space=pl.ANY)] * len(after),
        out_specs=tuple(pl.BlockSpec(memory_space=pltpu.VMEM) for _ in outs),
        scratch_shapes=scratch,
        compiler_params=pltpu.CompilerParams(vmem_limit_bytes=32 << 20),
        cost_estimate=pl.CostEstimate(flops=flops, bytes_accessed=moved, transcendentals=0),
    )(*args, *after)


def body(tokens, w_input, b_input, w_output, b_output):
    features, units = w_input.shape
    wide = features + features // QUARTERS
    rows = MAIN + LEFT
    weights = (w_input, b_input, w_output)
    packed = jax.ShapeDtypeStruct((MAIN, wide), jnp.bfloat16)
    sums = jax.ShapeDtypeStruct((rows, features), jnp.float32)
    block = (pltpu.VMEM((rows, features), jnp.bfloat16),)
    flops = 4 * rows * features * units

    (copies,) = call(copies_kernel, (packed,), (tokens,))
    mine = exchange_z(copies)
    up1 = along_y(mine, 1)
    (own,) = call(own_kernel, (sums,), (mine,) + weights, block, flops)
    up1, own = lax.optimization_barrier((up1, own))
    up2 = along_y(up1, 1)
    down1 = along_y(mine, -1)
    back = []
    for away, k in ((up1, -1), (down1, 1), (up2, -2)):
        (part,) = call(away_kernel, (packed,), (away,) + weights, block, flops, (own,))
        back.append(along_y(part, k))
    total, outgoing = call(add_kernel, (sums, packed), (own, *back))
    got = exchange_z(outgoing)
    (out,) = call(
        last_kernel,
        (jax.ShapeDtypeStruct((EIGHT + REST, features), jnp.float32),),
        (total, got, b_output),
    )
    return out


def solution(mesh):
    fine = Mesh(mesh.devices.reshape(X, YH, CORES, YL, Z), NAMES)
    mp = ("y_lo", "z")
    return jax.shard_map(
        body,
        mesh=fine,
        in_specs=(P(NAMES, None), P(None, mp), P(mp), P(mp, None), P()),
        out_specs=P(NAMES, None),
        check_vma=False,
    )
```

```python
import jax
import jax.numpy as jnp
from jax import lax
from jax.experimental import pallas as pl
from jax.experimental.pallas import tpu as pltpu
from jax.sharding import Mesh, PartitionSpec as P

X, YH, CORES, YL, Z = 4, 2, 2, 4, 8
Y = YH * YL
NAMES = ("x", "y_hi", "core", "y_lo", "z")

EIGHT, REST, QUARTERS = 8, 2, 4
MAIN, LEFT = EIGHT * Z, REST * Z


def pairs(step):
    out = []
    for i in range(X * Y * CORES * Z):
        rest, z = divmod(i, Z)
        rest, yl = divmod(rest, YL)
        rest, core = divmod(rest, CORES)
        x, yh = divmod(rest, YH)
        x2, y2, c2, z2 = step(x, yh * YL + yl, core, z)
        yh2, yl2 = divmod(y2 % Y, YL)
        out.append((i, (((x2 * YH + yh2) * CORES + c2) * YL + yl2) * Z + z2 % Z))
    return out


def along_y(block, k):
    return lax.ppermute(block, NAMES, pairs(lambda x, y, c, z: (x, y + k * (1 - 2 * c), c, z)))


def exchange_z(blocks):
    return lax.all_to_all(blocks.reshape(Z, EIGHT, -1), "z", 0, 0, tiled=True).reshape(MAIN, -1)


def picks(q):
    row = lax.broadcasted_iota(jnp.int32, (LEFT, MAIN), 0)
    col = lax.broadcasted_iota(jnp.int32, (LEFT, MAIN), 1)
    return (col == QUARTERS * row + q).astype(jnp.bfloat16)


def puts(q):
    row = lax.broadcasted_iota(jnp.int32, (MAIN, LEFT), 0)
    col = lax.broadcasted_iota(jnp.int32, (MAIN, LEFT), 1)
    return (row == QUARTERS * col + q).astype(jnp.bfloat16)


def dot(a, b):
    return jnp.dot(a, b, preferred_element_type=jnp.float32)


def copies_kernel(tokens, out):
    features = tokens.shape[1]
    part = features // QUARTERS
    rows = tokens[...].astype(jnp.float32)
    rest = [
        rows[EIGHT + r : EIGHT + r + 1, q * part : (q + 1) * part] for r in range(REST) for q in range(QUARTERS)
    ]
    out[:, :features] = jnp.concatenate([rows[:EIGHT]] * Z, 0).astype(jnp.bfloat16)
    out[:, features:] = jnp.concatenate(rest * Z, 0).astype(jnp.bfloat16)


def expand(packed, block):
    features = block.shape[1]
    part = features // QUARTERS
    block[:MAIN] = packed[:, :features]
    left = packed[:, features:]
    for q in range(QUARTERS):
        block[MAIN:, q * part : (q + 1) * part] = dot(picks(q), left).astype(jnp.bfloat16)


def gelu(pre):
    return (0.5 * pre * (1.0 + lax.erf(pre * (0.5**0.5)))).astype(jnp.bfloat16)


def hidden_of(packed, w_input, b_input, block):
    expand(packed, block)
    return gelu(dot(block[...], w_input[...]) + b_input[...].reshape(1, -1))


def away_kernel(packed, w_input, b_input, w_output, earlier, out, block):
    hidden = hidden_of(packed, w_input, b_input, block)
    features = w_output.shape[1]
    part = features // QUARTERS
    left = jnp.zeros((MAIN, part), jnp.float32)
    for q in range(QUARTERS):
        at = slice(q * part, (q + 1) * part)
        sums = dot(hidden, w_output[:, at])
        out[:, at] = sums[:MAIN].astype(jnp.bfloat16)
        left = left + dot(puts(q), sums[MAIN:].astype(jnp.bfloat16))
    out[:, features:] = left.astype(jnp.bfloat16)


def own_kernel(packed, w_input, b_input, w_output, out, w_input_near, b_input_near, w_output_near, block, arrived):
    features = w_input.shape[0]
    part = features // QUARTERS
    quarters = [slice(q * part, (q + 1) * part) for q in range(QUARTERS)]
    moves = [pltpu.make_async_copy(b_input, b_input_near, arrived.at[2 * QUARTERS])]
    moves += [pltpu.make_async_copy(w_input.at[at], w_input_near.at[at], arrived.at[q]) for q, at in enumerate(quarters)]
    deep = w_output.shape[0] // QUARTERS
    moves += [
        pltpu.make_async_copy(
            w_output.at[pl.ds(q * deep, deep)], w_output_near.at[pl.ds(q * deep, deep)], arrived.at[QUARTERS + q]
        )
        for q in range(QUARTERS)
    ]
    for move in moves:
        move.start()
    expand(packed, block)
    moves[0].wait()
    pre = b_input_near[...].reshape(1, -1)
    for q, at in enumerate(quarters):
        moves[1 + q].wait()
        pre = pre + dot(block[:, at], w_input_near[at])
    hidden = gelu(pre)
    for move in moves[1 + QUARTERS :]:
        move.wait()
    for at in quarters:
        out[:, at] = dot(hidden, w_output_near[:, at])


def add_kernel(own, one, two, three, total, packed):
    features = own.shape[1]
    part = features // QUARTERS
    terms = (one, two, three)
    main = own[:MAIN]
    for term in terms:
        main = main + term[:, :features].astype(jnp.float32)
    total[:MAIN] = main
    packed[:, :features] = main.astype(jnp.bfloat16)
    left = jnp.zeros((MAIN, part), jnp.float32)
    for q in range(QUARTERS):
        at = slice(q * part, (q + 1) * part)
        sums = own[MAIN:, at]
        for term in terms:
            sums = sums + dot(picks(q), term[:, features:])
        total[MAIN:, at] = sums
        left = left + dot(puts(q), sums.astype(jnp.bfloat16))
    packed[:, features:] = left.astype(jnp.bfloat16)


def last_kernel(total, got, b_output, out):
    features = total.shape[1]
    part = features // QUARTERS
    me = lax.axis_index("z")
    bias = b_output[...].reshape(1, -1)
    summed = jnp.zeros((EIGHT, got.shape[1]), jnp.float32)
    others = got[...].astype(jnp.float32)
    for z in range(Z):
        summed = summed + jnp.where(me == z, 0.0, others[z * EIGHT : (z + 1) * EIGHT])
    at = pl.multiple_of(me * EIGHT, EIGHT)
    out[:EIGHT] = summed[:, :features] + total[pl.ds(at, EIGHT)] + bias
    rows = lax.broadcasted_iota(jnp.int32, (LEFT, 1), 0)
    for r in range(REST):
        mine = jnp.where(rows == me * REST + r, total[MAIN:], 0.0).sum(0, keepdims=True) + bias
        for q in range(QUARTERS):
            cols = slice(q * part, (q + 1) * part)
            row = QUARTERS * r + q
            out[EIGHT + r : EIGHT + r + 1, cols] = mine[:, cols] + summed[row : row + 1, features:]


def call(kernel, outs, args, scratch=(), flops=0, after=(), in_hbm=()):
    moved = sum(a.size * a.dtype.itemsize for a in args)
    return pl.pallas_call(
        kernel,
        out_shape=outs,
        in_specs=[pl.BlockSpec(memory_space=pltpu.HBM if i in in_hbm else pltpu.VMEM) for i in range(len(args))] + [pl.BlockSpec(memory_space=pl.ANY)] * len(after),
        out_specs=tuple(pl.BlockSpec(memory_space=pltpu.VMEM) for _ in outs),
        scratch_shapes=scratch,
        compiler_params=pltpu.CompilerParams(vmem_limit_bytes=32 << 20),
        cost_estimate=pl.CostEstimate(flops=flops, bytes_accessed=moved, transcendentals=0),
    )(*args, *after)


def body(tokens, w_input, b_input, w_output, b_output):
    features, units = w_input.shape
    wide = features + features // QUARTERS
    rows = MAIN + LEFT
    weights = (w_input, b_input, w_output)
    inside = tuple(pltpu.VMEM(w.shape, w.dtype) for w in weights)
    packed = jax.ShapeDtypeStruct((MAIN, wide), jnp.bfloat16)
    sums = jax.ShapeDtypeStruct((rows, features), jnp.float32)
    block = (pltpu.VMEM((rows, features), jnp.bfloat16),)
    flops = 4 * rows * features * units

    (copies,) = call(copies_kernel, (packed,), (tokens,))
    mine = exchange_z(copies)
    up1 = along_y(mine, 1)
    own, *weights = call(
        own_kernel,
        (sums,) + inside,
        (mine,) + tuple(pltpu.with_memory_space_constraint(w, pltpu.HBM) for w in weights),
        block + (pltpu.SemaphoreType.DMA((2 * QUARTERS + 1,)),),
        flops,
        in_hbm=(1, 2, 3),
    )
    weights = tuple(pltpu.with_memory_space_constraint(w, pltpu.VMEM) for w in weights)
    up1, own = lax.optimization_barrier((up1, own))
    up2 = along_y(up1, 1)
    down1 = along_y(mine, -1)
    back = []
    for away, k in ((up1, -1), (down1, 1), (up2, -2)):
        (part,) = call(away_kernel, (packed,), (away,) + weights, block, flops, (own,))
        back.append(along_y(part, k))
    total, outgoing = call(add_kernel, (sums, packed), (own, *back))
    got = exchange_z(outgoing)
    (out,) = call(
        last_kernel,
        (jax.ShapeDtypeStruct((EIGHT + REST, features), jnp.float32),),
        (total, got, b_output),
    )
    return out


def solution(mesh):
    fine = Mesh(mesh.devices.reshape(X, YH, CORES, YL, Z), NAMES)
    mp = ("y_lo", "z")
    return jax.shard_map(
        body,
        mesh=fine,
        in_specs=(P(NAMES, None), P(None, mp), P(mp), P(mp, None), P()),
        out_specs=P(NAMES, None),
        check_vma=False,
    )
```

```python
import jax
import jax.numpy as jnp
from jax import lax
from jax.experimental import pallas as pl
from jax.experimental.pallas import tpu as pltpu
from jax.sharding import Mesh, PartitionSpec as P

X, YH, CORES, YL, Z = 4, 2, 2, 4, 8
Y = YH * YL
NAMES = ("x", "y_hi", "core", "y_lo", "z")

EIGHT, REST, QUARTERS = 8, 2, 4
MAIN, LEFT = EIGHT * Z, REST * Z


def pairs(step):
    out = []
    for i in range(X * Y * CORES * Z):
        rest, z = divmod(i, Z)
        rest, yl = divmod(rest, YL)
        rest, core = divmod(rest, CORES)
        x, yh = divmod(rest, YH)
        x2, y2, c2, z2 = step(x, yh * YL + yl, core, z)
        yh2, yl2 = divmod(y2 % Y, YL)
        out.append((i, (((x2 * YH + yh2) * CORES + c2) * YL + yl2) * Z + z2 % Z))
    return out


def along_y(block, k):
    return lax.ppermute(block, NAMES, pairs(lambda x, y, c, z: (x, y + k * (1 - 2 * c), c, z)))


def exchange_z(blocks):
    return lax.all_to_all(blocks.reshape(Z, EIGHT, -1), "z", 0, 0, tiled=True).reshape(MAIN, -1)


def picks(q):
    row = lax.broadcasted_iota(jnp.int32, (LEFT, MAIN), 0)
    col = lax.broadcasted_iota(jnp.int32, (LEFT, MAIN), 1)
    return (col == QUARTERS * row + q).astype(jnp.bfloat16)


def puts(q):
    row = lax.broadcasted_iota(jnp.int32, (MAIN, LEFT), 0)
    col = lax.broadcasted_iota(jnp.int32, (MAIN, LEFT), 1)
    return (row == QUARTERS * col + q).astype(jnp.bfloat16)


def dot(a, b):
    return jnp.dot(a, b, preferred_element_type=jnp.float32)


def copies_kernel(source, out, tokens, arrived):
    move = pltpu.make_async_copy(source, tokens, arrived)
    move.start()
    move.wait()
    features = tokens.shape[1]
    part = features // QUARTERS
    rows = tokens[...].astype(jnp.float32)
    rest = [
        rows[EIGHT + r : EIGHT + r + 1, q * part : (q + 1) * part] for r in range(REST) for q in range(QUARTERS)
    ]
    out[:, :features] = jnp.concatenate([rows[:EIGHT]] * Z, 0).astype(jnp.bfloat16)
    out[:, features:] = jnp.concatenate(rest * Z, 0).astype(jnp.bfloat16)


def expand(packed, block):
    features = block.shape[1]
    part = features // QUARTERS
    block[:MAIN] = packed[:, :features]
    left = packed[:, features:]
    for q in range(QUARTERS):
        block[MAIN:, q * part : (q + 1) * part] = dot(picks(q), left).astype(jnp.bfloat16)


def gelu(pre):
    return (0.5 * pre * (1.0 + lax.erf(pre * (0.5**0.5)))).astype(jnp.bfloat16)


def hidden_of(packed, w_input, b_input, block):
    expand(packed, block)
    return gelu(dot(block[...], w_input[...]) + b_input[...].reshape(1, -1))


def away_kernel(packed, w_input, b_input, w_output, out, block):
    hidden = hidden_of(packed, w_input, b_input, block)
    features = w_output.shape[1]
    part = features // QUARTERS
    left = jnp.zeros((MAIN, part), jnp.float32)
    for q in range(QUARTERS):
        at = slice(q * part, (q + 1) * part)
        sums = dot(hidden, w_output[:, at])
        out[:, at] = sums[:MAIN].astype(jnp.bfloat16)
        left = left + dot(puts(q), sums[MAIN:].astype(jnp.bfloat16))
    out[:, features:] = left.astype(jnp.bfloat16)


def fetch_kernel(w_input, b_input, w_output, w_input_near, b_input_near, w_output_near, arrived):
    moves = [pltpu.make_async_copy(b_input, b_input_near, arrived.at[2 * QUARTERS])]
    for i, (far, near) in enumerate(((w_input, w_input_near), (w_output, w_output_near))):
        deep = far.shape[0] // QUARTERS
        moves += [
            pltpu.make_async_copy(
                far.at[pl.ds(q * deep, deep)], near.at[pl.ds(q * deep, deep)], arrived.at[i * QUARTERS + q]
            )
            for q in range(QUARTERS)
        ]
    for move in moves:
        move.start()
    for move in moves:
        move.wait()


def own_kernel(packed, w_input, b_input, w_output, out, block):
    hidden = hidden_of(packed, w_input, b_input, block)
    part = w_output.shape[1] // QUARTERS
    for q in range(QUARTERS):
        at = slice(q * part, (q + 1) * part)
        out[:, at] = dot(hidden, w_output[:, at])


def near_kernel(own, one, two, total):
    features = own.shape[1]
    part = features // QUARTERS
    terms = (one, two)
    main = own[:MAIN]
    for term in terms:
        main = main + term[:, :features].astype(jnp.float32)
    total[:MAIN] = main
    for q in range(QUARTERS):
        at = slice(q * part, (q + 1) * part)
        sums = own[MAIN:, at]
        for term in terms:
            sums = sums + dot(picks(q), term[:, features:])
        total[MAIN:, at] = sums


def add_kernel(own, far, total, packed):
    features = own.shape[1]
    part = features // QUARTERS
    terms = (far,)
    main = own[:MAIN]
    for term in terms:
        main = main + term[:, :features].astype(jnp.float32)
    total[:MAIN] = main
    packed[:, :features] = main.astype(jnp.bfloat16)
    left = jnp.zeros((MAIN, part), jnp.float32)
    for q in range(QUARTERS):
        at = slice(q * part, (q + 1) * part)
        sums = own[MAIN:, at]
        for term in terms:
            sums = sums + dot(picks(q), term[:, features:])
        total[MAIN:, at] = sums
        left = left + dot(puts(q), sums.astype(jnp.bfloat16))
    packed[:, features:] = left.astype(jnp.bfloat16)


def last_kernel(total, got, b_output, out):
    features = total.shape[1]
    part = features // QUARTERS
    me = lax.axis_index("z")
    bias = b_output[...].reshape(1, -1)
    summed = jnp.zeros((EIGHT, got.shape[1]), jnp.float32)
    others = got[...].astype(jnp.float32)
    for z in range(Z):
        summed = summed + jnp.where(me == z, 0.0, others[z * EIGHT : (z + 1) * EIGHT])
    at = pl.multiple_of(me * EIGHT, EIGHT)
    out[:EIGHT] = summed[:, :features] + total[pl.ds(at, EIGHT)] + bias
    rows = lax.broadcasted_iota(jnp.int32, (LEFT, 1), 0)
    for r in range(REST):
        mine = jnp.where(rows == me * REST + r, total[MAIN:], 0.0).sum(0, keepdims=True) + bias
        for q in range(QUARTERS):
            cols = slice(q * part, (q + 1) * part)
            row = QUARTERS * r + q
            out[EIGHT + r : EIGHT + r + 1, cols] = mine[:, cols] + summed[row : row + 1, features:]


def call(kernel, outs, args, scratch=(), flops=0, after=(), in_hbm=()):
    moved = sum(a.size * a.dtype.itemsize for a in args)
    return pl.pallas_call(
        kernel,
        out_shape=outs,
        in_specs=[pl.BlockSpec(memory_space=pltpu.HBM if i in in_hbm else pltpu.VMEM) for i in range(len(args))] + [pl.BlockSpec(memory_space=pl.ANY)] * len(after),
        out_specs=tuple(pl.BlockSpec(memory_space=pltpu.VMEM) for _ in outs),
        scratch_shapes=scratch,
        compiler_params=pltpu.CompilerParams(vmem_limit_bytes=32 << 20),
        cost_estimate=pl.CostEstimate(flops=flops, bytes_accessed=moved, transcendentals=0),
    )(*args, *after)


def body(tokens, w_input, b_input, w_output, b_output):
    features, units = w_input.shape
    wide = features + features // QUARTERS
    rows = MAIN + LEFT
    weights = (w_input, b_input, w_output)
    inside = tuple(pltpu.VMEM(w.shape, w.dtype) for w in weights)
    packed = jax.ShapeDtypeStruct((MAIN, wide), jnp.bfloat16)
    sums = jax.ShapeDtypeStruct((rows, features), jnp.float32)
    block = (pltpu.VMEM((rows, features), jnp.bfloat16),)
    flops = 4 * rows * features * units

    (copies,) = call(
        copies_kernel,
        (packed,),
        (pltpu.with_memory_space_constraint(tokens, pltpu.HBM),),
        (pltpu.VMEM(tokens.shape, tokens.dtype), pltpu.SemaphoreType.DMA),
        in_hbm=(0,),
    )
    mine = exchange_z(copies)
    up1 = along_y(mine, 1)
    weights = call(
        fetch_kernel,
        inside,
        tuple(pltpu.with_memory_space_constraint(w, pltpu.HBM) for w in weights),
        (pltpu.SemaphoreType.DMA((2 * QUARTERS + 1,)),),
        in_hbm=(0, 1, 2),
    )
    up1, *weights = lax.optimization_barrier((up1, *weights))
    weights = tuple(pltpu.with_memory_space_constraint(w, pltpu.VMEM) for w in weights)
    (own,) = call(own_kernel, (sums,), (mine,) + weights, block, flops)
    up2 = along_y(up1, 1)
    down1 = along_y(mine, -1)
    back = []
    (part,) = call(away_kernel, (packed,), (up1,) + weights, block, flops)
    back.append(along_y(part, -1))
    down1, part = lax.optimization_barrier((down1, part))
    (part,) = call(away_kernel, (packed,), (down1,) + weights, block, flops)
    back.append(along_y(part, 1))
    (part,) = call(away_kernel, (packed,), (up2,) + weights, block, flops)
    back.append(along_y(part, -2))
    (near,) = call(near_kernel, (sums,), (own, *back[:2]))
    total, outgoing = call(add_kernel, (sums, packed), (near, back[2]))
    got = exchange_z(outgoing)
    (out,) = call(
        last_kernel,
        (jax.ShapeDtypeStruct((EIGHT + REST, features), jnp.float32),),
        (total, got, b_output),
    )
    return out


def solution(mesh):
    fine = Mesh(mesh.devices.reshape(X, YH, CORES, YL, Z), NAMES)
    mp = ("y_lo", "z")
    return jax.shard_map(
        body,
        mesh=fine,
        in_specs=(P(NAMES, None), P(None, mp), P(mp), P(mp, None), P()),
        out_specs=P(NAMES, None),
        check_vma=False,
    )
```

```python
import jax
import jax.numpy as jnp
from jax import lax
from jax.experimental import pallas as pl
from jax.experimental.pallas import tpu as pltpu
from jax.sharding import Mesh, PartitionSpec as P

X, YH, CORES, YL, Z = 4, 2, 2, 4, 8
Y = YH * YL
NAMES = ("x", "y_hi", "core", "y_lo", "z")

EIGHT, REST, QUARTERS = 8, 2, 4
MAIN, LEFT = EIGHT * Z, REST * Z


def pairs(step):
    out = []
    for i in range(X * Y * CORES * Z):
        rest, z = divmod(i, Z)
        rest, yl = divmod(rest, YL)
        rest, core = divmod(rest, CORES)
        x, yh = divmod(rest, YH)
        x2, y2, c2, z2 = step(x, yh * YL + yl, core, z)
        yh2, yl2 = divmod(y2 % Y, YL)
        out.append((i, (((x2 * YH + yh2) * CORES + c2) * YL + yl2) * Z + z2 % Z))
    return out


def along_y(block, k):
    return lax.ppermute(block, NAMES, pairs(lambda x, y, c, z: (x, y + k * (1 - 2 * c), c, z)))


def exchange_z(blocks):
    return lax.all_to_all(blocks.reshape(Z, EIGHT, -1), "z", 0, 0, tiled=True).reshape(MAIN, -1)


def picks(q):
    row = lax.broadcasted_iota(jnp.int32, (LEFT, MAIN), 0)
    col = lax.broadcasted_iota(jnp.int32, (LEFT, MAIN), 1)
    return (col == QUARTERS * row + q).astype(jnp.bfloat16)


def puts(q):
    row = lax.broadcasted_iota(jnp.int32, (MAIN, LEFT), 0)
    col = lax.broadcasted_iota(jnp.int32, (MAIN, LEFT), 1)
    return (row == QUARTERS * col + q).astype(jnp.bfloat16)


def dot(a, b):
    return jnp.dot(a, b, preferred_element_type=jnp.float32)


def copies_kernel(tokens, out):
    features = tokens.shape[1]
    part = features // QUARTERS
    rows = tokens[...].astype(jnp.float32)
    rest = [
        rows[EIGHT + r : EIGHT + r + 1, q * part : (q + 1) * part] for r in range(REST) for q in range(QUARTERS)
    ]
    out[:, :features] = jnp.concatenate([rows[:EIGHT]] * Z, 0).astype(jnp.bfloat16)
    out[:, features:] = jnp.concatenate(rest * Z, 0).astype(jnp.bfloat16)


def expand(packed, block):
    features = block.shape[1]
    part = features // QUARTERS
    block[:MAIN] = packed[:, :features]
    left = packed[:, features:]
    for q in range(QUARTERS):
        block[MAIN:, q * part : (q + 1) * part] = dot(picks(q), left).astype(jnp.bfloat16)


def gelu(pre):
    return (0.5 * pre * (1.0 + lax.erf(pre * (0.5**0.5)))).astype(jnp.bfloat16)


def hidden_of(packed, w_input, b_input, block):
    expand(packed, block)
    return gelu(dot(block[...], w_input[...]) + b_input[...].reshape(1, -1))


def away_kernel(packed, w_input, b_input, w_output, out, block):
    hidden = hidden_of(packed, w_input, b_input, block)
    features = w_output.shape[1]
    part = features // QUARTERS
    left = jnp.zeros((MAIN, part), jnp.float32)
    for q in range(QUARTERS):
        at = slice(q * part, (q + 1) * part)
        sums = dot(hidden, w_output[:, at])
        out[:, at] = sums[:MAIN].astype(jnp.bfloat16)
        left = left + dot(puts(q), sums[MAIN:].astype(jnp.bfloat16))
    out[:, features:] = left.astype(jnp.bfloat16)


def fetch_kernel(w_input, b_input, w_output, w_input_near, b_input_near, w_output_near, arrived):
    moves = [pltpu.make_async_copy(b_input, b_input_near, arrived.at[2 * QUARTERS])]
    for i, (far, near) in enumerate(((w_input, w_input_near), (w_output, w_output_near))):
        deep = far.shape[0] // QUARTERS
        moves += [
            pltpu.make_async_copy(
                far.at[pl.ds(q * deep, deep)], near.at[pl.ds(q * deep, deep)], arrived.at[i * QUARTERS + q]
            )
            for q in range(QUARTERS)
        ]
    for move in moves:
        move.start()
    for move in moves:
        move.wait()


def own_kernel(packed, w_input, b_input, w_output, out, block):
    hidden = hidden_of(packed, w_input, b_input, block)
    part = w_output.shape[1] // QUARTERS
    for q in range(QUARTERS):
        at = slice(q * part, (q + 1) * part)
        out[:, at] = dot(hidden, w_output[:, at])


def near_kernel(own, one, two, total):
    features = own.shape[1]
    part = features // QUARTERS
    terms = (one, two)
    main = own[:MAIN]
    for term in terms:
        main = main + term[:, :features].astype(jnp.float32)
    total[:MAIN] = main
    for q in range(QUARTERS):
        at = slice(q * part, (q + 1) * part)
        sums = own[MAIN:, at]
        for term in terms:
            sums = sums + dot(picks(q), term[:, features:])
        total[MAIN:, at] = sums


def add_kernel(own, far, total, packed):
    features = own.shape[1]
    part = features // QUARTERS
    terms = (far,)
    main = own[:MAIN]
    for term in terms:
        main = main + term[:, :features].astype(jnp.float32)
    total[:MAIN] = main
    packed[:, :features] = main.astype(jnp.bfloat16)
    left = jnp.zeros((MAIN, part), jnp.float32)
    for q in range(QUARTERS):
        at = slice(q * part, (q + 1) * part)
        sums = own[MAIN:, at]
        for term in terms:
            sums = sums + dot(picks(q), term[:, features:])
        total[MAIN:, at] = sums
        left = left + dot(puts(q), sums.astype(jnp.bfloat16))
    packed[:, features:] = left.astype(jnp.bfloat16)


def last_kernel(total, got, b_output, out):
    features = total.shape[1]
    part = features // QUARTERS
    me = lax.axis_index("z")
    bias = b_output[...].reshape(1, -1)
    summed = jnp.zeros((EIGHT, got.shape[1]), jnp.float32)
    others = got[...].astype(jnp.float32)
    for z in range(Z):
        summed = summed + jnp.where(me == z, 0.0, others[z * EIGHT : (z + 1) * EIGHT])
    at = pl.multiple_of(me * EIGHT, EIGHT)
    out[:EIGHT] = summed[:, :features] + total[pl.ds(at, EIGHT)] + bias
    rows = lax.broadcasted_iota(jnp.int32, (LEFT, 1), 0)
    for r in range(REST):
        mine = jnp.where(rows == me * REST + r, total[MAIN:], 0.0).sum(0, keepdims=True) + bias
        for q in range(QUARTERS):
            cols = slice(q * part, (q + 1) * part)
            row = QUARTERS * r + q
            out[EIGHT + r : EIGHT + r + 1, cols] = mine[:, cols] + summed[row : row + 1, features:]


def call(kernel, outs, args, scratch=(), flops=0, after=(), in_hbm=()):
    moved = sum(a.size * a.dtype.itemsize for a in args)
    return pl.pallas_call(
        kernel,
        out_shape=outs,
        in_specs=[pl.BlockSpec(memory_space=pltpu.HBM if i in in_hbm else pltpu.VMEM) for i in range(len(args))] + [pl.BlockSpec(memory_space=pl.ANY)] * len(after),
        out_specs=tuple(pl.BlockSpec(memory_space=pltpu.VMEM) for _ in outs),
        scratch_shapes=scratch,
        compiler_params=pltpu.CompilerParams(vmem_limit_bytes=32 << 20),
        cost_estimate=pl.CostEstimate(flops=flops, bytes_accessed=moved, transcendentals=0),
    )(*args, *after)


def body(tokens, w_input, b_input, w_output, b_output):
    features, units = w_input.shape
    wide = features + features // QUARTERS
    rows = MAIN + LEFT
    weights = (w_input, b_input, w_output)
    inside = tuple(pltpu.VMEM(w.shape, w.dtype) for w in weights)
    packed = jax.ShapeDtypeStruct((MAIN, wide), jnp.bfloat16)
    sums = jax.ShapeDtypeStruct((rows, features), jnp.float32)
    block = (pltpu.VMEM((rows, features), jnp.bfloat16),)
    flops = 4 * rows * features * units

    (copies,) = call(copies_kernel, (packed,), (tokens,))
    mine = exchange_z(copies)
    up1 = along_y(mine, 1)
    weights = call(
        fetch_kernel,
        inside,
        tuple(pltpu.with_memory_space_constraint(w, pltpu.HBM) for w in weights),
        (pltpu.SemaphoreType.DMA((2 * QUARTERS + 1,)),),
        in_hbm=(0, 1, 2),
    )
    up1, *weights = lax.optimization_barrier((up1, *weights))
    weights = tuple(pltpu.with_memory_space_constraint(w, pltpu.VMEM) for w in weights)
    (own,) = call(own_kernel, (sums,), (mine,) + weights, block, flops)
    up2 = along_y(up1, 1)
    down1 = along_y(mine, -1)
    back = []
    (part,) = call(away_kernel, (packed,), (up1,) + weights, block, flops)
    back.append(along_y(part, -1))
    down1, part = lax.optimization_barrier((down1, part))
    (part,) = call(away_kernel, (packed,), (down1,) + weights, block, flops)
    back.append(along_y(part, 1))
    (part,) = call(away_kernel, (packed,), (up2,) + weights, block, flops)
    back.append(along_y(part, -2))
    (near,) = call(near_kernel, (sums,), (own, *back[:2]))
    total, outgoing = call(add_kernel, (sums, packed), (near, back[2]))
    got = exchange_z(outgoing)
    (out,) = call(
        last_kernel,
        (jax.ShapeDtypeStruct((EIGHT + REST, features), jnp.float32),),
        (total, got, b_output),
    )
    return out


def solution(mesh):
    fine = Mesh(mesh.devices.reshape(X, YH, CORES, YL, Z), NAMES)
    mp = ("y_lo", "z")
    return jax.shard_map(
        body,
        mesh=fine,
        in_specs=(P(NAMES, None), P(None, mp), P(mp), P(mp, None), P()),
        out_specs=P(NAMES, None),
        check_vma=False,
    )
```

```python
import jax
import jax.numpy as jnp
from jax import lax
from jax.experimental import pallas as pl
from jax.experimental.pallas import tpu as pltpu
from jax.sharding import Mesh, PartitionSpec as P

X, YH, CORES, YL, Z = 4, 2, 2, 4, 8
Y = YH * YL
NAMES = ("x", "y_hi", "core", "y_lo", "z")

EIGHT, REST, QUARTERS = 8, 2, 4
MAIN, LEFT = EIGHT * Z, REST * Z


def pairs(step):
    out = []
    for i in range(X * Y * CORES * Z):
        rest, z = divmod(i, Z)
        rest, yl = divmod(rest, YL)
        rest, core = divmod(rest, CORES)
        x, yh = divmod(rest, YH)
        x2, y2, c2, z2 = step(x, yh * YL + yl, core, z)
        yh2, yl2 = divmod(y2 % Y, YL)
        out.append((i, (((x2 * YH + yh2) * CORES + c2) * YL + yl2) * Z + z2 % Z))
    return out


def along_y(block, k):
    return lax.ppermute(block, NAMES, pairs(lambda x, y, c, z: (x, y + k * (1 - 2 * c), c, z)))


def exchange_z(blocks):
    return lax.all_to_all(blocks.reshape(Z, EIGHT, -1), "z", 0, 0, tiled=True).reshape(MAIN, -1)


def picks(q):
    row = lax.broadcasted_iota(jnp.int32, (LEFT, MAIN), 0)
    col = lax.broadcasted_iota(jnp.int32, (LEFT, MAIN), 1)
    return (col == QUARTERS * row + q).astype(jnp.bfloat16)


def puts(q):
    row = lax.broadcasted_iota(jnp.int32, (MAIN, LEFT), 0)
    col = lax.broadcasted_iota(jnp.int32, (MAIN, LEFT), 1)
    return (row == QUARTERS * col + q).astype(jnp.bfloat16)


def dot(a, b):
    return jnp.dot(a, b, preferred_element_type=jnp.float32)


def copies_kernel(tokens, out):
    features = tokens.shape[1]
    part = features // QUARTERS
    rows = tokens[...].astype(jnp.float32)
    rest = [
        rows[EIGHT + r : EIGHT + r + 1, q * part : (q + 1) * part] for r in range(REST) for q in range(QUARTERS)
    ]
    out[:, :features] = jnp.concatenate([rows[:EIGHT]] * Z, 0).astype(jnp.bfloat16)
    out[:, features:] = jnp.concatenate(rest * Z, 0).astype(jnp.bfloat16)


def expand(packed, block):
    features = block.shape[1]
    part = features // QUARTERS
    block[:MAIN] = packed[:, :features]
    left = packed[:, features:]
    for q in range(QUARTERS):
        block[MAIN:, q * part : (q + 1) * part] = dot(picks(q), left).astype(jnp.bfloat16)


def gelu(pre):
    return (0.5 * pre * (1.0 + lax.erf(pre * (0.5**0.5)))).astype(jnp.bfloat16)


def hidden_of(packed, w_input, b_input, block):
    expand(packed, block)
    return gelu(dot(block[...], w_input[...]) + b_input[...].reshape(1, -1))


def away_kernel(packed, w_input, b_input, w_output, earlier, out, block):
    hidden = hidden_of(packed, w_input, b_input, block)
    features = w_output.shape[1]
    part = features // QUARTERS
    left = jnp.zeros((MAIN, part), jnp.float32)
    for q in range(QUARTERS):
        at = slice(q * part, (q + 1) * part)
        sums = dot(hidden, w_output[:, at])
        out[:, at] = sums[:MAIN].astype(jnp.bfloat16)
        left = left + dot(puts(q), sums[MAIN:].astype(jnp.bfloat16))
    out[:, features:] = left.astype(jnp.bfloat16)


def far_kernel(packed, w_input, b_input, w_output, earlier, low, high, block, out):
    away_kernel(packed, w_input, b_input, w_output, earlier, out, block)
    low[...] = out[: MAIN // 2]
    high[...] = out[MAIN // 2 :]


def own_kernel(packed, w_input, b_input, w_output, out, w_input_near, b_input_near, w_output_near, block, arrived):
    features = w_input.shape[0]
    part = features // QUARTERS
    quarters = [slice(q * part, (q + 1) * part) for q in range(QUARTERS)]
    moves = [pltpu.make_async_copy(b_input, b_input_near, arrived.at[2 * QUARTERS])]
    moves += [pltpu.make_async_copy(w_input.at[at], w_input_near.at[at], arrived.at[q]) for q, at in enumerate(quarters)]
    deep = w_output.shape[0] // QUARTERS
    moves += [
        pltpu.make_async_copy(
            w_output.at[pl.ds(q * deep, deep)], w_output_near.at[pl.ds(q * deep, deep)], arrived.at[QUARTERS + q]
        )
        for q in range(QUARTERS)
    ]
    for move in moves:
        move.start()
    expand(packed, block)
    moves[0].wait()
    pre = b_input_near[...].reshape(1, -1)
    for q, at in enumerate(quarters):
        moves[1 + q].wait()
        pre = pre + dot(block[:, at], w_input_near[at])
    hidden = gelu(pre)
    for move in moves[1 + QUARTERS :]:
        move.wait()
    for at in quarters:
        out[:, at] = dot(hidden, w_output_near[:, at])


def add_kernel(own, one, two, low, high, total, packed, three):
    features = own.shape[1]
    part = features // QUARTERS
    three[: MAIN // 2] = low[...]
    three[MAIN // 2 :] = high[...]
    terms = (one, two, three)
    main = own[:MAIN]
    for term in terms:
        main = main + term[:, :features].astype(jnp.float32)
    total[:MAIN] = main
    packed[:, :features] = main.astype(jnp.bfloat16)
    left = jnp.zeros((MAIN, part), jnp.float32)
    for q in range(QUARTERS):
        at = slice(q * part, (q + 1) * part)
        sums = own[MAIN:, at]
        for term in terms:
            sums = sums + dot(picks(q), term[:, features:])
        total[MAIN:, at] = sums
        left = left + dot(puts(q), sums.astype(jnp.bfloat16))
    packed[:, features:] = left.astype(jnp.bfloat16)


def last_kernel(total, got, b_output, out):
    features = total.shape[1]
    part = features // QUARTERS
    me = lax.axis_index("z")
    bias = b_output[...].reshape(1, -1)
    summed = jnp.zeros((EIGHT, got.shape[1]), jnp.float32)
    others = got[...].astype(jnp.float32)
    for z in range(Z):
        summed = summed + jnp.where(me == z, 0.0, others[z * EIGHT : (z + 1) * EIGHT])
    at = pl.multiple_of(me * EIGHT, EIGHT)
    out[:EIGHT] = summed[:, :features] + total[pl.ds(at, EIGHT)] + bias
    rows = lax.broadcasted_iota(jnp.int32, (LEFT, 1), 0)
    for r in range(REST):
        mine = jnp.where(rows == me * REST + r, total[MAIN:], 0.0).sum(0, keepdims=True) + bias
        for q in range(QUARTERS):
            cols = slice(q * part, (q + 1) * part)
            row = QUARTERS * r + q
            out[EIGHT + r : EIGHT + r + 1, cols] = mine[:, cols] + summed[row : row + 1, features:]


def call(kernel, outs, args, scratch=(), flops=0, after=(), in_hbm=()):
    moved = sum(a.size * a.dtype.itemsize for a in args)
    return pl.pallas_call(
        kernel,
        out_shape=outs,
        in_specs=[pl.BlockSpec(memory_space=pltpu.HBM if i in in_hbm else pltpu.VMEM) for i in range(len(args))] + [pl.BlockSpec(memory_space=pl.ANY)] * len(after),
        out_specs=tuple(pl.BlockSpec(memory_space=pltpu.VMEM) for _ in outs),
        scratch_shapes=scratch,
        compiler_params=pltpu.CompilerParams(vmem_limit_bytes=32 << 20),
        cost_estimate=pl.CostEstimate(flops=flops, bytes_accessed=moved, transcendentals=0),
    )(*args, *after)


def body(tokens, w_input, b_input, w_output, b_output):
    features, units = w_input.shape
    wide = features + features // QUARTERS
    rows = MAIN + LEFT
    weights = (w_input, b_input, w_output)
    inside = tuple(pltpu.VMEM(w.shape, w.dtype) for w in weights)
    packed = jax.ShapeDtypeStruct((MAIN, wide), jnp.bfloat16)
    sums = jax.ShapeDtypeStruct((rows, features), jnp.float32)
    block = (pltpu.VMEM((rows, features), jnp.bfloat16),)
    flops = 4 * rows * features * units

    (copies,) = call(copies_kernel, (packed,), (tokens,))
    mine = exchange_z(copies)
    up1 = along_y(mine, 1)
    own, *weights = call(
        own_kernel,
        (sums,) + inside,
        (mine,) + tuple(pltpu.with_memory_space_constraint(w, pltpu.HBM) for w in weights),
        block + (pltpu.SemaphoreType.DMA((2 * QUARTERS + 1,)),),
        flops,
        in_hbm=(1, 2, 3),
    )
    weights = tuple(pltpu.with_memory_space_constraint(w, pltpu.VMEM) for w in weights)
    up1, own = lax.optimization_barrier((up1, own))
    up2 = along_y(up1, 1)
    down1 = along_y(mine, -1)
    back = []
    for away, k in ((up1, -1), (down1, 1)):
        (part,) = call(away_kernel, (packed,), (away,) + weights, block, flops, (own,))
        back.append(along_y(part, k))
    half = jax.ShapeDtypeStruct((MAIN // 2, wide), jnp.bfloat16)
    low, high = call(far_kernel, (half, half), (up2,) + weights, block + (pltpu.VMEM(packed.shape, packed.dtype),), flops, (own,))
    back += [along_y(low, -2), along_y(high, -2)]
    total, outgoing = call(add_kernel, (sums, packed), (own, *back), (pltpu.VMEM(packed.shape, packed.dtype),))
    got = exchange_z(outgoing)
    (out,) = call(
        last_kernel,
        (jax.ShapeDtypeStruct((EIGHT + REST, features), jnp.float32),),
        (total, got, b_output),
    )
    return out


def solution(mesh):
    fine = Mesh(mesh.devices.reshape(X, YH, CORES, YL, Z), NAMES)
    mp = ("y_lo", "z")
    return jax.shard_map(
        body,
        mesh=fine,
        in_specs=(P(NAMES, None), P(None, mp), P(mp), P(mp, None), P()),
        out_specs=P(NAMES, None),
        check_vma=False,
    )
```
